128 devices in a mesh: wave: 16 (over y_hi, x, core), lev: 8 (over y_lo, z).
Axes of the slice: x: 4, y: 4 (y_hi: 2, y_lo: 2; y = y_hi * 2 + y_lo), z: 4, core: 2. Of those that a mesh axis runs over, the one named last changes fastest.
Arguments:
- spectral: bfloat16 [1280, 2, 2, 64, 1280], P('wave', None, None, 'lev'), may hold values from -0.125 to 0.125
- legendre: bfloat16 [1280, 64, 1280], P('wave'), may hold values from -0.15625 to 0.15625
- derivative: bfloat16 [1280, 64, 1280], P('wave'), may hold values from -0.15625 to 0.15625
- wave_order: int32 [1280], replicated, may hold values from 0 to 1279, each once
- lat_order: int32 [128], replicated, may hold values from 0 to 127, each once
- row_lengths: int32 [64], replicated, may hold values from 20 to 5136, as said below
- tile_map: int32 [48], replicated, may hold values from 0 to 47, each once
Outputs:
- grid: bfloat16 [128, 3, 64, 6144], P('wave', None, None, 'lev')
- vort_max: float32 [], replicated
The draws below stay inside these ranges and needn't reach their ends.
Inputs may be any that keep to these rules, and one draw needn't show every extreme that they name: `wave_order`: each of 0 to 1279 once. `lat_order`: each of 0 to 127 once. `row_lengths`: each is 4 j + 20 for a whole number j below 1280; the largest, 5136, occurs in every draw. `tile_map`: each of 0 to 47 once.
All inputs are finite; a program needn't handle non-finite values.
Results may differ from the reference program's by a relative error of at most 0.0061.
Values may be sent and summed in bfloat16 or wider, within the bound.
No kernel may reach another device: no remote copies, remote signals or barrier semaphores. Data moves between devices by JAX's collectives and lax.ppermute only.
A program may use at most 192 MiB of HBM per device.

```python
import jax
import jax.numpy as jnp
from jax import lax

NM = 1280
HEMI = 1280
LATP = 64
TILE = 128
LEV = 64
ROWS = 128
NT = 48
NP = 6144


def draw_row_lengths(key, part):
    first_key, second_key = jax.random.split(jax.random.fold_in(key, 17))
    distance = jax.random.randint(first_key, (LATP,), 0, HEMI)
    longest = jax.random.randint(second_key, (), 0, LATP)
    distance = jnp.where(jnp.arange(LATP) == longest, HEMI - 1, distance)
    return (4 * distance + 20).astype(jnp.int32)


def block_scale(key, extent, pieces, least, largest):
    loudness, own = 1.0, jax.random.fold_in(key, 6)
    for axis_at, shards_of in pieces:
        steps = jnp.exp(jax.random.uniform(jax.random.fold_in(own, axis_at), (shards_of,), jnp.float32, least / len(pieces), largest / len(pieces)))
        loudness = loudness * jnp.repeat(steps, extent[axis_at] // shards_of).reshape([-1 if axis == axis_at else 1 for axis in range(len(extent))])
    return loudness


def scatter_about(key, shape, width, most, cuts=(), kind=jnp.bfloat16):
    drawn = width * jax.random.normal(key, shape, jnp.float32)
    if cuts:
        drawn = drawn * block_scale(key, shape, cuts, -0.22, 0.18)
    return jnp.clip(drawn, -most, most).astype(kind)


def setup_inputs(seed: int = 0) -> dict:
    seeds = jax.random.split(jax.random.key(seed), 8)
    return {
        "spectral": scatter_about(seeds[0], (NM, 2, 2, LEV, NM), ((2 * NM) ** -0.5), 0.125, ((0, 16), (3, 8))),
        "legendre": scatter_about(seeds[1], (NM, LATP, NM), NM ** -0.5, 0.15625, ((0, 16),)),
        "derivative": scatter_about(seeds[2], (NM, LATP, NM), NM ** -0.5, 0.15625, ((0, 16),)),
        "wave_order": jax.random.permutation(seeds[3], NM).astype(jnp.int32),
        "lat_order": jax.random.permutation(seeds[4], ROWS).astype(jnp.int32),
        "row_lengths": draw_row_lengths(jax.random.fold_in(seeds[7], 71), 0),
        "tile_map": jax.random.permutation(seeds[6], NT).astype(jnp.int32),
    }


TWO_PI = 6.283185307179586


def spectral_operands(coefficients, wave_numbers):
    n_index = jnp.arange(NM, dtype=jnp.int32)
    n_float = n_index.astype(jnp.float32)
    factor = jnp.where(n_index > 0, -float(NM) / jnp.maximum(n_float * (n_float + 1.0), 1.0), 0.0).astype(jnp.float32)
    relative = coefficients[:, 0].astype(jnp.float32)
    diverge = coefficients[:, 1].astype(jnp.float32)
    stream = relative * factor
    potential = diverge * factor
    wave_col = wave_numbers.astype(jnp.float32)[:, None, None]
    value_parts = jnp.stack([relative[:, 0], relative[:, 1], -wave_col * potential[:, 1], wave_col * potential[:, 0], -wave_col * stream[:, 1], wave_col * stream[:, 0]], axis=1)
    slope_parts = jnp.stack([-stream[:, 0], -stream[:, 1], potential[:, 0], potential[:, 1]], axis=1)
    parity = jnp.where((n_index[None, :] + wave_numbers[:, None]) % 2 == 0, 1.0, -1.0).astype(jnp.float32)[:, None, None, :]
    active = (n_index[None, :] >= wave_numbers[:, None]).astype(jnp.float32)[:, None, None, :]
    value_op = jnp.stack([value_parts * active, value_parts * parity * active], axis=1)
    slope_op = jnp.stack([slope_parts * active, -slope_parts * parity * active], axis=1)
    slot_count = coefficients.shape[0]
    levels = coefficients.shape[3]
    return value_op.reshape(slot_count, 12 * levels, NM).astype(jnp.bfloat16), slope_op.reshape(slot_count, 8 * levels, NM).astype(jnp.bfloat16)


def legendre_block(coefficients, legendre, derivative, wave_numbers):
    value_op, slope_op = spectral_operands(coefficients, wave_numbers)
    on_value = jnp.einsum("kin,kcn->kic", legendre.astype(jnp.float32), value_op.astype(jnp.float32))
    on_slope = jnp.einsum("kin,kcn->kic", derivative.astype(jnp.float32), slope_op.astype(jnp.float32))
    slot_count = legendre.shape[0]
    pair_count = legendre.shape[1]
    levels = coefficients.shape[3]
    on_value = on_value.reshape(slot_count, pair_count, 2, 3, 2, levels)
    on_slope = on_slope.reshape(slot_count, pair_count, 2, 2, 2, levels)
    summed = jnp.concatenate([on_value[:, :, :, :1], on_value[:, :, :, 1:] + on_slope], axis=3)
    summed = summed.transpose(0, 2, 1, 4, 3, 5).reshape(slot_count, 2 * pair_count, 2, 3, levels)
    return summed.astype(jnp.bfloat16)


def row_transform(coef_row, wave_numbers, longitudes, length):
    wave_col = wave_numbers[:, None]
    lon_row = longitudes[None, :]
    turned = (wave_col * lon_row) % length
    angles = (turned.astype(jnp.float32) * TWO_PI) / length.astype(jnp.float32)
    weight = jnp.where(wave_col == 0, 1.0, 2.0).astype(jnp.float32)
    active = (2 * wave_col < length) & (lon_row < length)
    real_part = jnp.where(active, weight * jnp.cos(angles), 0.0)
    imag_part = jnp.where(active, -weight * jnp.sin(angles), 0.0)
    trig_table = jnp.stack([real_part, imag_part], axis=1).astype(jnp.bfloat16)
    return jnp.einsum("spc,spk->ck", coef_row.astype(jnp.float32), trig_table.astype(jnp.float32))


def reference(spectral, legendre, derivative, wave_order, lat_order, row_lengths, tile_map):
    slot_group = 16

    def one_group(group_index):
        offset = group_index * slot_group
        coefficients = lax.dynamic_slice_in_dim(spectral, offset, slot_group, 0)
        values_in = lax.dynamic_slice_in_dim(legendre, offset, slot_group, 0)
        slopes_in = lax.dynamic_slice_in_dim(derivative, offset, slot_group, 0)
        numbers = lax.dynamic_slice_in_dim(wave_order, offset, slot_group, 0)
        return legendre_block(coefficients, values_in, slopes_in, numbers)

    fourier = lax.map(one_group, jnp.arange(NM // slot_group, dtype=jnp.int32))
    fourier = fourier.reshape(NM, 2 * LATP, 2, 3, LEV)
    all_longitudes = (tile_map[:, None] * TILE + jnp.arange(TILE, dtype=jnp.int32)[None, :]).reshape(-1)

    def one_row(out_slot):
        lat_row = lat_order[out_slot]
        length = row_lengths[lat_row % LATP]
        coef_row = lax.dynamic_index_in_dim(fourier, lat_row, 1, keepdims=False)
        values = row_transform(coef_row.reshape(NM, 2, 3 * LEV), wave_order, all_longitudes, length)
        grid_row = values.astype(jnp.bfloat16).reshape(3, LEV, NP)
        return grid_row, jnp.max(grid_row[0].astype(jnp.float32))

    grid_values, peaks = lax.map(one_row, jnp.arange(2 * LATP, dtype=jnp.int32))
    return grid_values, jnp.max(peaks)
```

```python
import functools

import jax
import jax.numpy as jnp
from jax import lax
from jax.experimental import pallas as pl
from jax.experimental.pallas import tpu as pltpu
from jax.sharding import PartitionSpec as P

NM = 1280
TILE = 128
GROUP = 16
SPAN = 256
BLOCKS = 24
PAIRS = 11
MIB = 1024 * 1024


def swap_lanes(parts, low_bit, lane):
    count = len(parts)
    bit = 1
    while bit < count:
        shift = bit * low_bit
        clear = (lane & shift) == 0
        fresh = list(parts)
        for at in range(count):
            if at & bit == 0:
                low, high = parts[at], parts[at | bit]
                fresh[at] = jnp.where(clear, low, pltpu.roll(high, shift, 1))
                fresh[at | bit] = jnp.where(clear, pltpu.roll(low, TILE - shift, 1), high)
        parts = fresh
        bit *= 2
    return parts


def legendre_kernel(step_slots, waves, spectral, legendre, derivative, factor, permute, out, held):
    group, part = pl.program_id(0), pl.program_id(1)
    degree = lax.broadcasted_iota(jnp.int32, (8, NM), 1)
    lane = lax.broadcasted_iota(jnp.int32, (48, TILE), 1)
    scale = factor[...]
    for at in range(step_slots):
        wave = waves[group * GROUP + part * step_slots + at]
        live = degree >= wave
        even = (degree + wave) % 2 == 0
        keep_even = jnp.where(live & even, 1.0, 0.0)
        keep_odd = jnp.where(live & ~even, 1.0, 0.0)
        vort_re = spectral[at, 0, 0].astype(jnp.float32)
        vort_im = spectral[at, 0, 1].astype(jnp.float32)
        div_re = spectral[at, 1, 0].astype(jnp.float32)
        div_im = spectral[at, 1, 1].astype(jnp.float32)
        rows = []
        for keep in (keep_even, keep_odd):
            scaled = scale * keep
            rows += [
                vort_re * keep,
                vort_im * keep,
                vort_re * scaled,
                vort_im * scaled,
                div_re * scaled,
                div_im * scaled,
            ]
        operand = jnp.concatenate(rows, axis=0).astype(jnp.bfloat16)
        both = jnp.concatenate([legendre[at], derivative[at]], axis=0)
        sums = lax.dot_general(
            operand, both, (((1,), (1,)), ((), ())), preferred_element_type=jnp.float32
        )
        even_sum, odd_sum = sums[:48], sums[48:]
        north = even_sum + odd_sum
        south = even_sum - odd_sum
        left = lane < 64
        value = jnp.where(left, north, pltpu.roll(south, 64, 1))
        slope = jnp.where(left, pltpu.roll(north, 64, 1), -south)
        wave_float = wave.astype(jnp.float32)
        held[part * step_slots + at] = jnp.concatenate(
            [
                value[0:8],
                -wave_float * value[40:48] - slope[16:24],
                -wave_float * value[24:32] + slope[32:40],
                value[8:16],
                wave_float * value[32:40] - slope[24:32],
                wave_float * value[16:24] + slope[40:48],
            ],
            axis=0,
        )

    @pl.when(part == GROUP // step_slots - 1)
    def _():
        rounded = held[...].reshape(GROUP * 48, TILE).astype(jnp.bfloat16)
        placed = jnp.dot(rounded, permute[...], preferred_element_type=jnp.float32)
        parts = [placed[48 * at : 48 * at + 48] for at in range(GROUP)]
        for at, block in enumerate(swap_lanes(parts, 1, lane)):
            out[at, 0] = block.astype(jnp.bfloat16)


def legendre_stage(spectral, legendre, derivative, own_waves, lat_order):
    slots = spectral.shape[0]
    groups = slots // GROUP
    step_slots = 4
    steps = GROUP // step_slots
    degree = jnp.arange(NM, dtype=jnp.int32).astype(jnp.float32)
    factor = jnp.where(degree > 0, -float(NM) / jnp.maximum(degree * (degree + 1.0), 1.0), 0.0)
    factor = jnp.broadcast_to(factor[None, :], (8, NM))
    lane_row = lat_order.reshape(16, 8).T.reshape(TILE)
    permute = (jnp.arange(TILE, dtype=jnp.int32)[:, None] == lane_row[None, :]).astype(jnp.bfloat16)
    return pl.pallas_call(
        functools.partial(legendre_kernel, step_slots),
        grid_spec=pltpu.PrefetchScalarGridSpec(
            num_scalar_prefetch=1,
            grid=(groups, steps),
            in_specs=[
                pl.BlockSpec((step_slots, 2, 2, 8, NM), lambda g, k, w: (g * steps + k, 0, 0, 0, 0)),
                pl.BlockSpec((step_slots, 64, NM), lambda g, k, w: (g * steps + k, 0, 0)),
                pl.BlockSpec((step_slots, 64, NM), lambda g, k, w: (g * steps + k, 0, 0)),
                pl.BlockSpec((8, NM), lambda g, k, w: (0, 0)),
                pl.BlockSpec((TILE, TILE), lambda g, k, w: (0, 0)),
            ],
            out_specs=pl.BlockSpec((16, 1, 48, TILE), lambda g, k, w: (0, g, 0, 0)),
            scratch_shapes=[pltpu.VMEM((GROUP, 48, TILE), jnp.float32)],
        ),
        out_shape=jax.ShapeDtypeStruct((16, groups, 48, TILE), jnp.bfloat16),
        compiler_params=pltpu.CompilerParams(vmem_limit_bytes=40 * MIB),
        cost_estimate=pl.CostEstimate(
            flops=slots * 96 * 128 * NM * 2, bytes_accessed=slots * 160 * NM * 2, transcendentals=0
        ),
    )(own_waves, spectral, legendre, derivative, factor, permute)


def turn_parts(product, length, inverse):
    turned = product - jnp.floor(product * inverse) * length
    turn = turned * inverse
    quarter = jnp.floor(turn * 4.0 + 0.5)
    angle = (turn - quarter * 0.25) * 6.283185307179586
    square = angle * angle
    sine = angle * (1.0 + square * (-1.0 / 6 + square * (1.0 / 120 + square * (-1.0 / 5040))))
    cosine = 1.0 + square * (
        -0.5 + square * (1.0 / 24 + square * (-1.0 / 720 + square * (1.0 / 40320)))
    )
    which = quarter.astype(jnp.int32)
    odd = (which & 1) == 1
    cos_sign = jnp.where(((which + 1) & 2) == 0, 1.0, -1.0)
    sin_sign = jnp.where((which & 2) == 0, 1.0, -1.0)
    return cos_sign * jnp.where(odd, sine, cosine), sin_sign * jnp.where(odd, cosine, sine)


def table_kernel(lengths, waves, table, base):
    length = lengths[pl.program_id(0)].astype(jnp.float32)
    spread = jnp.full((8, NM), length)
    inverse = (1.0 / spread)[:1]
    wave = waves[...]
    step = lax.broadcasted_iota(jnp.int32, (16, NM), 0).astype(jnp.float32)
    fine_cos, fine_sin = turn_parts(step * wave, length, inverse)
    coarse_cos, coarse_sin = turn_parts(step * wave * 16.0, length, inverse)
    for at in range(16):
        one_cos, one_sin = coarse_cos[at : at + 1], coarse_sin[at : at + 1]
        rows = slice(16 * at, 16 * at + 16)
        table[0, rows, :NM] = (one_cos * fine_cos - one_sin * fine_sin).astype(jnp.bfloat16)
        table[0, rows, NM:] = (-one_sin * fine_cos - one_cos * fine_sin).astype(jnp.bfloat16)
    block = lax.broadcasted_iota(jnp.int32, (BLOCKS, NM), 0).astype(jnp.float32)
    base_cos, base_sin = turn_parts(block * wave * float(SPAN), length, inverse)
    weight = jnp.where(wave == 0.0, 1.0, 2.0) * jnp.where(2.0 * wave < length, 1.0, 0.0)
    base[0, 0] = base_cos * weight
    base[0, 1] = base_sin * weight


def table_stage(lengths, wave_row):
    rows = lengths.shape[0]
    return pl.pallas_call(
        table_kernel,
        grid_spec=pltpu.PrefetchScalarGridSpec(
            num_scalar_prefetch=1,
            grid=(rows,),
            in_specs=[pl.BlockSpec((1, NM), lambda r, n: (0, 0))],
            out_specs=[
                pl.BlockSpec((1, SPAN, 2 * NM), lambda r, n: (r, 0, 0)),
                pl.BlockSpec((1, 2, BLOCKS, NM), lambda r, n: (r, 0, 0, 0)),
            ],
        ),
        out_shape=[
            jax.ShapeDtypeStruct((rows, SPAN, 2 * NM), jnp.bfloat16),
            jax.ShapeDtypeStruct((rows, 2, BLOCKS, NM), jnp.float32),
        ],
        compiler_params=pltpu.CompilerParams(vmem_limit_bytes=30 * MIB),
        cost_estimate=pl.CostEstimate(
            flops=rows * SPAN * NM * 10, bytes_accessed=rows * SPAN * NM * 5, transcendentals=0
        ),
    )(lengths, wave_row)


def fourier_kernel(lengths, slots, coeffs, table, base, out, highest, fields, turned, peak):
    row = pl.program_id(0)
    rows = pl.num_programs(0)
    lane = lax.broadcasted_iota(jnp.int32, (48, TILE), 1)

    @pl.when(row == 0)
    def _():
        peak[...] = jnp.zeros_like(peak)
        for group in range(5):
            for half in range(2):
                parts = [
                    coeffs[half * 8 + at, group].astype(jnp.float32) for at in range(8)
                ]
                tile = group * 2 + half
                for at, block in enumerate(swap_lanes(parts, 16, lane)):
                    fields[at, :, tile * TILE : tile * TILE + TILE] = block

    out[...] = jnp.zeros_like(out)
    length = lengths[row]
    column = lax.broadcasted_iota(jnp.int32, (24, TILE), 1)

    def one_group(first_pair):
        for pair in range(4):
            at_pair = first_pair + pair

            @pl.when(at_pair * (2 * SPAN) < length)
            def _():
                for chunk in range(5):
                    lanes = slice(chunk * 256, chunk * 256 + 256)
                    shifted = slice(NM + chunk * 256, NM + chunk * 256 + 256)
                    real = fields[row, 0:24, lanes]
                    imag = fields[row, 24:48, lanes]
                    turned_re, turned_im = [], []
                    for side in range(2):
                        cosine = base[0, 0, pl.ds(at_pair * 2 + side, 1), lanes]
                        sine = base[0, 1, pl.ds(at_pair * 2 + side, 1), lanes]
                        turned_re.append(real * cosine - imag * sine)
                        turned_im.append(real * sine + imag * cosine)
                    held = slice(pair * 48, pair * 48 + 48)
                    turned[held, lanes] = jnp.concatenate(turned_re, 0).astype(jnp.bfloat16)
                    turned[held, shifted] = jnp.concatenate(turned_im, 0).astype(jnp.bfloat16)

        values = lax.dot_general(
            turned[...], table[0], (((1,), (1,)), ((), ())), preferred_element_type=jnp.float32
        )
        for block in range(8):
            for side in range(2):
                tile = first_pair * 4 + block * 2 + side

                @pl.when(tile * TILE < length)
                def _():
                    piece = values[block * 24 : block * 24 + 24, side * TILE : side * TILE + TILE]
                    piece = jnp.where(column + tile * TILE < length, piece, 0.0)
                    rounded = piece.astype(jnp.bfloat16)
                    slot = slots[tile]
                    for field in range(3):
                        out[slot // 6, 0, slot % 6, field] = rounded[field * 8 : field * 8 + 8]
                    peak[...] = jnp.maximum(peak[...], rounded.astype(jnp.float32)[:8])

    for group in range(3):

        @pl.when(group * (8 * SPAN) < length)
        def _():
            one_group(group * 4)

    @pl.when(row == rows - 1)
    def _():
        highest[...] = jnp.full((8, TILE), jnp.max(peak[...]))


def fourier_stage(lengths, tile_slots, coeffs, table, base):
    rows = lengths.shape[0]
    return pl.pallas_call(
        fourier_kernel,
        grid_spec=pltpu.PrefetchScalarGridSpec(
            num_scalar_prefetch=2,
            grid=(rows,),
            in_specs=[
                pl.BlockSpec(coeffs.shape, lambda r, n, s: (0, 0, 0, 0)),
                pl.BlockSpec((1, SPAN, 2 * NM), lambda r, n, s: (r, 0, 0)),
                pl.BlockSpec((1, 2, BLOCKS, NM), lambda r, n, s: (r, 0, 0, 0)),
            ],
            out_specs=[
                pl.BlockSpec((8, 1, 6, 3, 8, TILE), lambda r, n, s: (0, r, 0, 0, 0, 0)),
                pl.BlockSpec((8, TILE), lambda r, n, s: (0, 0)),
            ],
            scratch_shapes=[
                pltpu.VMEM((rows, 48, NM), jnp.float32),
                pltpu.VMEM((192, 2 * NM), jnp.bfloat16),
                pltpu.VMEM((8, TILE), jnp.float32),
            ],
        ),
        out_shape=[
            jax.ShapeDtypeStruct((8, rows, 6, 3, 8, TILE), jnp.bfloat16),
            jax.ShapeDtypeStruct((8, TILE), jnp.float32),
        ],
        compiler_params=pltpu.CompilerParams(vmem_limit_bytes=40 * MIB),
        cost_estimate=pl.CostEstimate(
            flops=rows * 576 * 2 * NM * 256, bytes_accessed=rows * SPAN * NM * 5, transcendentals=0
        ),
    )(lengths, tile_slots, coeffs, table, base)


def shards(spectral, legendre, derivative, wave_order, lat_order, row_lengths, tile_map):
    wave_index = lax.axis_index("wave")
    slot_count = spectral.shape[0]
    own_waves = lax.dynamic_slice_in_dim(wave_order, wave_index * slot_count, slot_count)
    coeffs = legendre_stage(spectral, legendre, derivative, own_waves, lat_order)
    fourier = lax.all_to_all(coeffs, "wave", split_axis=0, concat_axis=0, tiled=True)

    row_ids = lax.dynamic_slice_in_dim(lat_order, wave_index * 8, 8)
    lengths = row_lengths[row_ids % 64]
    wave_row = wave_order.reshape(16, 5, GROUP).transpose(1, 0, 2).reshape(1, NM).astype(jnp.float32)
    table, base = table_stage(lengths, wave_row)
    tile_slots = jnp.zeros((48,), jnp.int32).at[tile_map].set(jnp.arange(48, dtype=jnp.int32))
    grid_part, highest = fourier_stage(lengths, tile_slots, fourier, table, base)
    received = lax.all_to_all(grid_part, "lev", split_axis=0, concat_axis=0, tiled=True)
    grid_values = received.transpose(1, 3, 0, 4, 2, 5).reshape(8, 3, 64, 768)
    for axis in ("lev", "wave"):
        count = lax.axis_size(axis)
        hop = 1
        while hop < count:
            pairs = [(at, at ^ hop) for at in range(count)]
            highest = jnp.maximum(highest, lax.ppermute(highest, axis, pairs))
            hop *= 2
    return (grid_values, highest[0, 0])


def solution(mesh):
    placed = (
        P("wave", None, None, "lev", None),
        P("wave", None, None),
        P("wave", None, None),
        P(),
        P(),
        P(),
        P(),
    )
    return jax.shard_map(
        shards,
        mesh=mesh,
        in_specs=placed,
        out_specs=(P("wave", None, None, "lev"), P()),
        check_vma=False,
    )
```

```python
import functools

import jax
import jax.numpy as jnp
from jax import lax
from jax.experimental import pallas as pl
from jax.experimental.pallas import tpu as pltpu
from jax.sharding import PartitionSpec as P

NM = 1280
TILE = 128
GROUP = 16
SPAN = 256
BLOCKS = 24
PAIRS = 11
BATCH = 4
MIB = 1024 * 1024


def swap_lanes(parts, low_bit, lane):
    count = len(parts)
    bit = 1
    while bit < count:
        shift = bit * low_bit
        clear = (lane & shift) == 0
        fresh = list(parts)
        for at in range(count):
            if at & bit == 0:
                low, high = parts[at], parts[at | bit]
                fresh[at] = jnp.where(clear, low, pltpu.roll(high, shift, 1))
                fresh[at | bit] = jnp.where(clear, pltpu.roll(low, TILE - shift, 1), high)
        parts = fresh
        bit *= 2
    return parts


def legendre_kernel(
    waves, spectral, legendre, derivative, factor, permute, out,
    spec_in, leg_in, der_in, sums, order, spec_sem, leg_sem, der_sem,
):
    slots = spectral.shape[0]
    lane = lax.broadcasted_iota(jnp.int32, (48, TILE), 1)
    half = TILE // 2
    cuts = NM // SPAN

    def copies(slot, cut):
        lanes = pl.ds(cut * SPAN, NM - cut * SPAN)
        return (
            pltpu.make_async_copy(
                legendre.at[slot, :, lanes], leg_in.at[slot, :, lanes], leg_sem.at[slot]
            ),
            pltpu.make_async_copy(
                derivative.at[slot, :, lanes], der_in.at[slot, :, lanes], der_sem.at[slot]
            ),
            pltpu.make_async_copy(
                spectral.at[slot, :, :, :, lanes], spec_in.at[slot, :, :, :, lanes], spec_sem.at[slot]
            ),
        )

    sizes = [jnp.int32(0)] * cuts
    for slot in range(slots):
        cut = waves[slot] // SPAN
        sizes = [size + (cut == at).astype(jnp.int32) for at, size in enumerate(sizes)]
    begins = [None] * cuts
    total = jnp.int32(0)
    for at in reversed(range(cuts)):
        begins[at] = total
        total = total + sizes[at]
    places = list(begins)
    for slot in range(slots):
        cut = waves[slot] // SPAN
        place = places[0]
        for at in range(1, cuts):
            place = jnp.where(cut == at, places[at], place)
        order[place] = slot
        places = [where + (cut == at).astype(jnp.int32) for at, where in enumerate(places)]

    for at in reversed(range(cuts)):

        def start(place, carry, at=at):
            for copy in copies(order[place], at):
                copy.start()
            return carry

        lax.fori_loop(begins[at], begins[at] + sizes[at], start, 0)

    for at in reversed(range(cuts)):
        first_lane = at * SPAN
        width = NM - first_lane
        end = begins[at] + sizes[at]

        def batch(step, carry, at=at, first_lane=first_lane, width=width, end=end):
            place = begins[at] + step * BATCH
            members = []
            for which in range(BATCH):
                slot = order[jnp.minimum(place + which, end - 1)]
                members.append(slot)

                @pl.when(place + which < end)
                def _(slot=slot):
                    for copy in copies(slot, at):
                        copy.wait()

            degree = lax.broadcasted_iota(jnp.int32, (8, width), 1) + first_lane
            scale = factor[:, first_lane:]
            results = []
            for slot in members:
                wave = waves[slot]
                live = degree >= wave
                odd = ((degree + wave) & 1) == 1
                keep_even = jnp.where(live & ~odd, 1.0, 0.0)
                keep_odd = jnp.where(live & odd, 1.0, 0.0)
                parts = [
                    spec_in[slot, field, side, :, first_lane:].astype(jnp.float32)
                    for field in range(2)
                    for side in range(2)
                ]
                rows = []
                for keep in (keep_even, keep_odd):
                    scaled = scale * keep
                    rows += [parts[0] * keep, parts[1] * keep]
                    rows += [part * scaled for part in parts]
                operand = jnp.concatenate(rows, axis=0).astype(jnp.bfloat16)
                both = jnp.concatenate(
                    [leg_in[slot, :, first_lane:], der_in[slot, :, first_lane:]], axis=0
                )
                results.append(
                    lax.dot_general(
                        operand, both, (((1,), (1,)), ((), ())), preferred_element_type=jnp.float32
                    )
                )
            for slot, result in zip(members, results):
                sums[slot] = result
            return carry

        lax.fori_loop(0, (sizes[at] + BATCH - 1) // BATCH, batch, 0)

    left = lane < half

    def finish(group, carry):
        parts = []
        for at in range(GROUP):
            slot = group * GROUP + at
            wave_float = waves[slot].astype(jnp.float32)
            even_sum, odd_sum = sums[slot, :48], sums[slot, 48:]
            north = even_sum + odd_sum
            south = even_sum - odd_sum
            value = jnp.where(left, north, pltpu.roll(south, half, 1))
            slope = jnp.where(left, pltpu.roll(north, half, 1), -south)
            parts.append(
                jnp.concatenate(
                    [
                        value[0:8],
                        -wave_float * value[40:48] - slope[16:24],
                        -wave_float * value[24:32] + slope[32:40],
                        value[8:16],
                        wave_float * value[32:40] - slope[24:32],
                        wave_float * value[16:24] + slope[40:48],
                    ],
                    axis=0,
                ).astype(jnp.bfloat16)
            )
        placed = jnp.dot(
            jnp.concatenate(parts, axis=0), permute[...], preferred_element_type=jnp.float32
        )
        parts = [placed[48 * at : 48 * at + 48] for at in range(GROUP)]
        for at, piece in enumerate(swap_lanes(parts, 1, lane)):
            out[at, group] = piece.astype(jnp.bfloat16)
        return carry

    lax.fori_loop(0, slots // GROUP, finish, 0)


def legendre_stage(spectral, legendre, derivative, own_waves, lat_order):
    slots = spectral.shape[0]
    groups = slots // GROUP
    degree = jnp.arange(NM, dtype=jnp.int32).astype(jnp.float32)
    factor = jnp.where(degree > 0, -float(NM) / jnp.maximum(degree * (degree + 1.0), 1.0), 0.0)
    factor = jnp.broadcast_to(factor[None, :], (8, NM))
    lane_row = lat_order.reshape(16, 8).T.reshape(TILE)
    permute = (jnp.arange(TILE, dtype=jnp.int32)[:, None] == lane_row[None, :]).astype(jnp.bfloat16)
    hbm = pl.BlockSpec(memory_space=pl.ANY)
    vmem = pl.BlockSpec(memory_space=pltpu.VMEM)
    return pl.pallas_call(
        legendre_kernel,
        in_specs=[pl.BlockSpec(memory_space=pltpu.SMEM), hbm, hbm, hbm, vmem, vmem],
        out_specs=vmem,
        scratch_shapes=[
            pltpu.VMEM((slots, 2, 2, 8, NM), jnp.bfloat16),
            pltpu.VMEM((slots, 64, NM), jnp.bfloat16),
            pltpu.VMEM((slots, 64, NM), jnp.bfloat16),
            pltpu.VMEM((slots, 96, TILE), jnp.float32),
            pltpu.SMEM((slots,), jnp.int32),
            pltpu.SemaphoreType.DMA((slots,)),
            pltpu.SemaphoreType.DMA((slots,)),
            pltpu.SemaphoreType.DMA((slots,)),
        ],
        out_shape=jax.ShapeDtypeStruct((16, groups, 48, TILE), jnp.bfloat16),
        compiler_params=pltpu.CompilerParams(vmem_limit_bytes=60 * MIB),
        cost_estimate=pl.CostEstimate(
            flops=slots * 96 * 128 * NM * 2, bytes_accessed=slots * 160 * NM * 2, transcendentals=0
        ),
    )(own_waves, spectral, legendre, derivative, factor, permute)


def turn_parts(product, length, inverse):
    turned = product - jnp.floor(product * inverse) * length
    turn = turned * inverse
    quarter = jnp.floor(turn * 4.0 + 0.5)
    angle = (turn - quarter * 0.25) * 6.283185307179586
    square = angle * angle
    sine = angle * (1.0 + square * (-1.0 / 6 + square * (1.0 / 120 + square * (-1.0 / 5040))))
    cosine = 1.0 + square * (
        -0.5 + square * (1.0 / 24 + square * (-1.0 / 720 + square * (1.0 / 40320)))
    )
    which = quarter.astype(jnp.int32)
    odd = (which & 1) == 1
    cos_sign = jnp.where(((which + 1) & 2) == 0, 1.0, -1.0)
    sin_sign = jnp.where((which & 2) == 0, 1.0, -1.0)
    return cos_sign * jnp.where(odd, sine, cosine), sin_sign * jnp.where(odd, cosine, sine)


def table_kernel(lengths, waves, table, base):
    length = lengths[pl.program_id(0)].astype(jnp.float32)
    spread = jnp.full((8, NM), length)
    inverse = (1.0 / spread)[:1]
    wave = waves[...]
    step = lax.broadcasted_iota(jnp.int32, (16, NM), 0).astype(jnp.float32)
    fine_cos, fine_sin = turn_parts(step * wave, length, inverse)
    coarse_cos, coarse_sin = turn_parts(step * wave * 16.0, length, inverse)
    for at in range(16):
        one_cos, one_sin = coarse_cos[at : at + 1], coarse_sin[at : at + 1]
        rows = slice(16 * at, 16 * at + 16)
        table[0, rows, :NM] = (one_cos * fine_cos - one_sin * fine_sin).astype(jnp.bfloat16)
        table[0, rows, NM:] = (-one_sin * fine_cos - one_cos * fine_sin).astype(jnp.bfloat16)
    block = lax.broadcasted_iota(jnp.int32, (BLOCKS, NM), 0).astype(jnp.float32)
    base_cos, base_sin = turn_parts(block * wave * float(SPAN), length, inverse)
    weight = jnp.where(wave == 0.0, 1.0, 2.0) * jnp.where(2.0 * wave < length, 1.0, 0.0)
    base[0, 0] = base_cos * weight
    base[0, 1] = base_sin * weight


def table_stage(lengths, wave_row):
    rows = lengths.shape[0]
    return pl.pallas_call(
        table_kernel,
        grid_spec=pltpu.PrefetchScalarGridSpec(
            num_scalar_prefetch=1,
            grid=(rows,),
            in_specs=[pl.BlockSpec((1, NM), lambda r, n: (0, 0))],
            out_specs=[
                pl.BlockSpec((1, SPAN, 2 * NM), lambda r, n: (r, 0, 0)),
                pl.BlockSpec((1, 2, BLOCKS, NM), lambda r, n: (r, 0, 0, 0)),
            ],
        ),
        out_shape=[
            jax.ShapeDtypeStruct((rows, SPAN, 2 * NM), jnp.bfloat16),
            jax.ShapeDtypeStruct((rows, 2, BLOCKS, NM), jnp.float32),
        ],
        compiler_params=pltpu.CompilerParams(vmem_limit_bytes=30 * MIB),
        cost_estimate=pl.CostEstimate(
            flops=rows * SPAN * NM * 10, bytes_accessed=rows * SPAN * NM * 5, transcendentals=0
        ),
    )(lengths, wave_row)


def fourier_kernel(lengths, slots, coeffs, table, base, out, highest, fields, turned, values, peak):
    row = pl.program_id(0)
    rows = pl.num_programs(0)
    lane = lax.broadcasted_iota(jnp.int32, (48, TILE), 1)

    @pl.when(row == 0)
    def _():
        peak[...] = jnp.zeros_like(peak)
        for group in range(5):
            for half in range(2):
                parts = [
                    coeffs[half * 8 + at, group].astype(jnp.float32) for at in range(8)
                ]
                tile = group * 2 + half
                for at, block in enumerate(swap_lanes(parts, 16, lane)):
                    fields[at, :, tile * TILE : tile * TILE + TILE] = block

    out[...] = jnp.zeros_like(out)
    length = lengths[row]
    pairs = (length + 2 * SPAN - 1) // (2 * SPAN)

    def turn(pair, carry):
        held = pl.ds(pl.multiple_of(pair * 48, 48), 48)
        for chunk in range(5):
            lanes = slice(chunk * 256, chunk * 256 + 256)
            shifted = slice(NM + chunk * 256, NM + chunk * 256 + 256)
            real = fields[row, 0:24, lanes]
            imag = fields[row, 24:48, lanes]
            turned_re, turned_im = [], []
            for side in range(2):
                cosine = base[0, 0, pl.ds(pair * 2 + side, 1), lanes]
                sine = base[0, 1, pl.ds(pair * 2 + side, 1), lanes]
                turned_re.append(real * cosine - imag * sine)
                turned_im.append(real * sine + imag * cosine)
            turned[held, lanes] = jnp.concatenate(turned_re, 0).astype(jnp.bfloat16)
            turned[held, shifted] = jnp.concatenate(turned_im, 0).astype(jnp.bfloat16)
        return carry

    lax.fori_loop(0, pairs, turn, 0)

    sizes = (2, 4, 6, 8, PAIRS)
    for at, size in enumerate(sizes):
        above = pairs > sizes[at - 1] if at else pairs > 0

        @pl.when(above & (pairs <= size))
        def _():
            values[: size * 48] = lax.dot_general(
                turned[: size * 48],
                table[0],
                (((1,), (1,)), ((), ())),
                preferred_element_type=jnp.float32,
            )

    column = lax.broadcasted_iota(jnp.int32, (24, TILE), 1)

    def store(pair, carry):
        best = peak[...]
        for block in range(2):
            for side in range(2):
                tile = pair * 4 + block * 2 + side
                piece = values[
                    pl.ds(pl.multiple_of(pair * 48 + block * 24, 8), 24),
                    side * TILE : side * TILE + TILE,
                ]
                piece = jnp.where(column + tile * TILE < length, piece, 0.0)
                rounded = piece.astype(jnp.bfloat16)
                slot = slots[tile]
                for field in range(3):
                    out[slot // 6, 0, slot % 6, field] = rounded[field * 8 : field * 8 + 8]
                best = jnp.maximum(best, rounded[:8].astype(jnp.float32))
        peak[...] = best
        return carry

    lax.fori_loop(0, pairs, store, 0)

    @pl.when(row == rows - 1)
    def _():
        highest[...] = jnp.full((8, TILE), jnp.max(peak[...]))


def fourier_stage(lengths, tile_slots, coeffs, table, base):
    rows = lengths.shape[0]
    return pl.pallas_call(
        fourier_kernel,
        grid_spec=pltpu.PrefetchScalarGridSpec(
            num_scalar_prefetch=2,
            grid=(rows,),
            in_specs=[
                pl.BlockSpec(coeffs.shape, lambda r, n, s: (0, 0, 0, 0)),
                pl.BlockSpec((1, SPAN, 2 * NM), lambda r, n, s: (r, 0, 0)),
                pl.BlockSpec((1, 2, BLOCKS, NM), lambda r, n, s: (r, 0, 0, 0)),
            ],
            out_specs=[
                pl.BlockSpec((8, 1, 6, 3, 8, TILE), lambda r, n, s: (0, r, 0, 0, 0, 0)),
                pl.BlockSpec((8, TILE), lambda r, n, s: (0, 0)),
            ],
            scratch_shapes=[
                pltpu.VMEM((rows, 48, NM), jnp.float32),
                pltpu.VMEM((PAIRS * 48, 2 * NM), jnp.bfloat16),
                pltpu.VMEM((PAIRS * 48, SPAN), jnp.float32),
                pltpu.VMEM((8, TILE), jnp.float32),
            ],
        ),
        out_shape=[
            jax.ShapeDtypeStruct((8, rows, 6, 3, 8, TILE), jnp.bfloat16),
            jax.ShapeDtypeStruct((8, TILE), jnp.float32),
        ],
        compiler_params=pltpu.CompilerParams(vmem_limit_bytes=40 * MIB),
        cost_estimate=pl.CostEstimate(
            flops=rows * 576 * 2 * NM * 256, bytes_accessed=rows * SPAN * NM * 5, transcendentals=0
        ),
    )(lengths, tile_slots, coeffs, table, base)


def shards(spectral, legendre, derivative, wave_order, lat_order, row_lengths, tile_map):
    wave_index = lax.axis_index("wave")
    slot_count = spectral.shape[0]
    own_waves = lax.dynamic_slice_in_dim(wave_order, wave_index * slot_count, slot_count)
    coeffs = legendre_stage(spectral, legendre, derivative, own_waves, lat_order)
    fourier = lax.all_to_all(coeffs, "wave", split_axis=0, concat_axis=0, tiled=True)

    row_ids = lax.dynamic_slice_in_dim(lat_order, wave_index * 8, 8)
    lengths = row_lengths[row_ids % 64]
    wave_row = wave_order.reshape(16, 5, GROUP).transpose(1, 0, 2).reshape(1, NM).astype(jnp.float32)
    table, base = table_stage(lengths, wave_row)
    tile_slots = jnp.zeros((48,), jnp.int32).at[tile_map].set(jnp.arange(48, dtype=jnp.int32))
    grid_part, highest = fourier_stage(lengths, tile_slots, fourier, table, base)
    received = lax.all_to_all(grid_part, "lev", split_axis=0, concat_axis=0, tiled=True)
    grid_values = received.transpose(1, 3, 0, 4, 2, 5).reshape(8, 3, 64, 768)
    highest = jnp.max(lax.all_gather(highest, "wave", axis=0), axis=0)
    hop = 1
    while hop < 8:
        pairs = [(at, at ^ hop) for at in range(8)]
        highest = jnp.maximum(highest, lax.ppermute(highest, "lev", pairs))
        hop *= 2
    return (grid_values, highest[0, 0])


def solution(mesh):
    placed = (
        P("wave", None, None, "lev", None),
        P("wave", None, None),
        P("wave", None, None),
        P(),
        P(),
        P(),
        P(),
    )
    return jax.shard_map(
        shards,
        mesh=mesh,
        in_specs=placed,
        out_specs=(P("wave", None, None, "lev"), P()),
        check_vma=False,
    )
```

```python
import functools

import jax
import jax.numpy as jnp
from jax import lax
from jax.experimental import pallas as pl
from jax.experimental.pallas import tpu as pltpu
from jax.sharding import PartitionSpec as P

NM = 1280
TILE = 128
GROUP = 16
SPAN = 256
BLOCKS = 24
PAIRS = 11
BATCH = 4
MIB = 1024 * 1024


def swap_lanes(parts, low_bit, lane):
    count = len(parts)
    bit = 1
    while bit < count:
        shift = bit * low_bit
        clear = (lane & shift) == 0
        fresh = list(parts)
        for at in range(count):
            if at & bit == 0:
                low, high = parts[at], parts[at | bit]
                fresh[at] = jnp.where(clear, low, pltpu.roll(high, shift, 1))
                fresh[at | bit] = jnp.where(clear, pltpu.roll(low, TILE - shift, 1), high)
        parts = fresh
        bit *= 2
    return parts


def legendre_kernel(
    all_waves, lat_row, spectral, legendre, derivative, out,
    spec_in, leg_in, der_in, sums, factor, permute, waves, order, spec_sem, leg_sem, der_sem,
):
    slots = spectral.shape[0]
    lane = lax.broadcasted_iota(jnp.int32, (48, TILE), 1)
    half = TILE // 2
    cuts = NM // SPAN

    def copies(slot, cut):
        lanes = pl.ds(cut * SPAN, NM - cut * SPAN)
        return (
            pltpu.make_async_copy(
                legendre.at[slot, :, lanes], leg_in.at[slot, :, lanes], leg_sem.at[slot]
            ),
            pltpu.make_async_copy(
                derivative.at[slot, :, lanes], der_in.at[slot, :, lanes], der_sem.at[slot]
            ),
            pltpu.make_async_copy(
                spectral.at[slot, :, :, :, lanes], spec_in.at[slot, :, :, :, lanes], spec_sem.at[slot]
            ),
        )

    own = lax.axis_index("wave") * slots
    sizes = [jnp.int32(0)] * cuts
    for slot in range(slots):
        waves[slot] = all_waves[own + slot]
        cut = waves[slot] // SPAN
        sizes = [size + (cut == at).astype(jnp.int32) for at, size in enumerate(sizes)]
    begins = [None] * cuts
    total = jnp.int32(0)
    for at in reversed(range(cuts)):
        begins[at] = total
        total = total + sizes[at]
    places = list(begins)
    for slot in range(slots):
        cut = waves[slot] // SPAN
        place = places[0]
        for at in range(1, cuts):
            place = jnp.where(cut == at, places[at], place)
        order[place] = slot
        places = [where + (cut == at).astype(jnp.int32) for at, where in enumerate(places)]

    for at in reversed(range(cuts)):

        def start(place, carry, at=at):
            for copy in copies(order[place], at):
                copy.start()
            return carry

        lax.fori_loop(begins[at], begins[at] + sizes[at], start, 0)

    number = lax.broadcasted_iota(jnp.int32, (8, NM), 1).astype(jnp.float32)
    factor[...] = jnp.where(number > 0, -float(NM) / jnp.maximum(number * (number + 1.0), 1.0), 0.0)
    down = lax.broadcasted_iota(jnp.int32, (TILE, TILE), 0)
    across = lax.broadcasted_iota(jnp.int32, (TILE, TILE), 1)
    at_row = jnp.where(down == lat_row[...], 1.0, 0.0).astype(jnp.bfloat16)
    at_lane = jnp.where(down == (across % 16) * 8 + across // 16, 1.0, 0.0).astype(jnp.bfloat16)
    permute[...] = jnp.dot(at_row, at_lane, preferred_element_type=jnp.float32).astype(jnp.bfloat16)

    for at in reversed(range(cuts)):
        first_lane = at * SPAN
        width = NM - first_lane
        end = begins[at] + sizes[at]

        def batch(step, carry, at=at, first_lane=first_lane, width=width, end=end):
            place = begins[at] + step * BATCH
            members = []
            for which in range(BATCH):
                slot = order[jnp.minimum(place + which, end - 1)]
                members.append(slot)

                @pl.when(place + which < end)
                def _(slot=slot):
                    for copy in copies(slot, at):
                        copy.wait()

            degree = lax.broadcasted_iota(jnp.int32, (8, width), 1) + first_lane
            scale = factor[:, first_lane:]
            results = []
            for slot in members:
                wave = waves[slot]
                live = degree >= wave
                odd = ((degree + wave) & 1) == 1
                keep_even = jnp.where(live & ~odd, 1.0, 0.0)
                keep_odd = jnp.where(live & odd, 1.0, 0.0)
                parts = [
                    spec_in[slot, field, side, :, first_lane:].astype(jnp.float32)
                    for field in range(2)
                    for side in range(2)
                ]
                rows = []
                for keep in (keep_even, keep_odd):
                    scaled = scale * keep
                    rows += [parts[0] * keep, parts[1] * keep]
                    rows += [part * scaled for part in parts]
                operand = jnp.concatenate(rows, axis=0).astype(jnp.bfloat16)
                both = jnp.concatenate(
                    [leg_in[slot, :, first_lane:], der_in[slot, :, first_lane:]], axis=0
                )
                results.append(
                    lax.dot_general(
                        operand, both, (((1,), (1,)), ((), ())), preferred_element_type=jnp.float32
                    )
                )
            for slot, result in zip(members, results):
                sums[slot] = result
            return carry

        lax.fori_loop(0, (sizes[at] + BATCH - 1) // BATCH, batch, 0)

    left = lane < half

    def finish(group, carry):
        parts = []
        for at in range(GROUP):
            slot = group * GROUP + at
            wave_float = waves[slot].astype(jnp.float32)
            even_sum, odd_sum = sums[slot, :48], sums[slot, 48:]
            north = even_sum + odd_sum
            south = even_sum - odd_sum
            value = jnp.where(left, north, pltpu.roll(south, half, 1))
            slope = jnp.where(left, pltpu.roll(north, half, 1), -south)
            parts.append(
                jnp.concatenate(
                    [
                        value[0:8],
                        -wave_float * value[40:48] - slope[16:24],
                        -wave_float * value[24:32] + slope[32:40],
                        value[8:16],
                        wave_float * value[32:40] - slope[24:32],
                        wave_float * value[16:24] + slope[40:48],
                    ],
                    axis=0,
                ).astype(jnp.bfloat16)
            )
        placed = jnp.dot(
            jnp.concatenate(parts, axis=0), permute[...], preferred_element_type=jnp.float32
        )
        placed = placed.astype(jnp.bfloat16)
        parts = [placed[48 * at : 48 * at + 48] for at in range(GROUP)]
        for at, piece in enumerate(swap_lanes(parts, 1, lane)):
            out[at, group] = piece
        return carry

    lax.fori_loop(0, slots // GROUP, finish, 0)


def legendre_stage(spectral, legendre, derivative, wave_order, lat_order):
    slots = spectral.shape[0]
    groups = slots // GROUP
    hbm = pl.BlockSpec(memory_space=pl.ANY)
    vmem = pl.BlockSpec(memory_space=pltpu.VMEM)
    return pl.pallas_call(
        legendre_kernel,
        in_specs=[pl.BlockSpec(memory_space=pltpu.SMEM), vmem, hbm, hbm, hbm],
        out_specs=vmem,
        scratch_shapes=[
            pltpu.VMEM((slots, 2, 2, 8, NM), jnp.bfloat16),
            pltpu.VMEM((slots, 64, NM), jnp.bfloat16),
            pltpu.VMEM((slots, 64, NM), jnp.bfloat16),
            pltpu.VMEM((slots, 96, TILE), jnp.float32),
            pltpu.VMEM((8, NM), jnp.float32),
            pltpu.VMEM((TILE, TILE), jnp.bfloat16),
            pltpu.SMEM((slots,), jnp.int32),
            pltpu.SMEM((slots,), jnp.int32),
            pltpu.SemaphoreType.DMA((slots,)),
            pltpu.SemaphoreType.DMA((slots,)),
            pltpu.SemaphoreType.DMA((slots,)),
        ],
        out_shape=jax.ShapeDtypeStruct((16, groups, 48, TILE), jnp.bfloat16),
        compiler_params=pltpu.CompilerParams(vmem_limit_bytes=60 * MIB),
        cost_estimate=pl.CostEstimate(
            flops=slots * 96 * 128 * NM * 2, bytes_accessed=slots * 160 * NM * 2, transcendentals=0
        ),
    )(wave_order, lat_order.reshape(1, TILE), spectral, legendre, derivative)


def turn_parts(product, length, inverse):
    turned = product - jnp.floor(product * inverse) * length
    turn = turned * inverse
    quarter = jnp.floor(turn * 4.0 + 0.5)
    angle = (turn - quarter * 0.25) * 6.283185307179586
    square = angle * angle
    sine = angle * (1.0 + square * (-1.0 / 6 + square * (1.0 / 120 + square * (-1.0 / 5040))))
    cosine = 1.0 + square * (
        -0.5 + square * (1.0 / 24 + square * (-1.0 / 720 + square * (1.0 / 40320)))
    )
    which = quarter.astype(jnp.int32)
    odd = (which & 1) == 1
    cos_sign = jnp.where(((which + 1) & 2) == 0, 1.0, -1.0)
    sin_sign = jnp.where((which & 2) == 0, 1.0, -1.0)
    return cos_sign * jnp.where(odd, sine, cosine), sin_sign * jnp.where(odd, cosine, sine)


def table_kernel(lengths, waves, table, base):
    wave = waves[...]
    step = lax.broadcasted_iota(jnp.int32, (16, NM), 0).astype(jnp.float32)
    block = lax.broadcasted_iota(jnp.int32, (BLOCKS, NM), 0).astype(jnp.float32)

    def one_row(row, carry):
        length = lengths[row].astype(jnp.float32)
        inverse = (1.0 / jnp.full((8, NM), length))[:1]
        fine_cos, fine_sin = turn_parts(step * wave, length, inverse)
        coarse_cos, coarse_sin = turn_parts(step * wave * 16.0, length, inverse)
        for at in range(16):
            one_cos, one_sin = coarse_cos[at : at + 1], coarse_sin[at : at + 1]
            span = slice(16 * at, 16 * at + 16)
            table[row, span, :NM] = (one_cos * fine_cos - one_sin * fine_sin).astype(jnp.bfloat16)
            table[row, span, NM:] = (-one_sin * fine_cos - one_cos * fine_sin).astype(jnp.bfloat16)
        base_cos, base_sin = turn_parts(block * wave * float(SPAN), length, inverse)
        weight = jnp.where(wave == 0.0, 1.0, 2.0) * jnp.where(2.0 * wave < length, 1.0, 0.0)
        base[row, 0] = base_cos * weight
        base[row, 1] = base_sin * weight
        return carry

    lax.fori_loop(0, table.shape[0], one_row, 0)


def table_stage(lengths, wave_row):
    rows = lengths.shape[0]
    vmem = pl.BlockSpec(memory_space=pltpu.VMEM)
    return pl.pallas_call(
        table_kernel,
        in_specs=[pl.BlockSpec(memory_space=pltpu.SMEM), vmem],
        out_specs=[vmem, vmem],
        out_shape=[
            jax.ShapeDtypeStruct((rows, SPAN, 2 * NM), jnp.bfloat16),
            jax.ShapeDtypeStruct((rows, 2, BLOCKS, NM), jnp.float32),
        ],
        compiler_params=pltpu.CompilerParams(vmem_limit_bytes=30 * MIB),
        cost_estimate=pl.CostEstimate(
            flops=rows * SPAN * NM * 40, bytes_accessed=rows * SPAN * NM * 5, transcendentals=0
        ),
    )(lengths, wave_row)


def fourier_kernel(
    lengths, slots, coeffs, table, base, out, highest,
    fields, turned, values, peak, staged, out_sem,
):
    rows = table.shape[0]
    lane = lax.broadcasted_iota(jnp.int32, (48, TILE), 1)
    column = lax.broadcasted_iota(jnp.int32, (24, TILE), 1)

    def result(row):
        return pltpu.make_async_copy(staged.at[:, row], out.at[:, row], out_sem.at[row])

    peak[...] = jnp.zeros_like(peak)
    for group in range(5):
        for half in range(2):
            parts = [coeffs[half * 8 + at, group] for at in range(8)]
            tile = group * 2 + half
            for at, block in enumerate(swap_lanes(parts, 16, lane)):
                fields[at, :, tile * TILE : tile * TILE + TILE] = block.astype(jnp.float32)

    def one_row(row, carry):
        length = lengths[row]
        pairs = (length + 2 * SPAN - 1) // (2 * SPAN)
        staged[:, row] = jnp.zeros((8, 6, 3, 8, TILE), jnp.bfloat16)
        sizes = (2, 4, 6, 8, PAIRS)
        for at, size in enumerate(sizes):
            above = pairs > sizes[at - 1] if at else pairs > 0

            @pl.when(above & (pairs <= size))
            def _(size=size):
                for chunk in range(5):
                    lanes = slice(chunk * 256, chunk * 256 + 256)
                    shifted = slice(NM + chunk * 256, NM + chunk * 256 + 256)
                    real = fields[row, 0:24, lanes]
                    imag = fields[row, 24:48, lanes]
                    for pair in range(size):
                        held = slice(pair * 48, pair * 48 + 48)
                        turned_re, turned_im = [], []
                        for side in range(2):
                            which = pair * 2 + side
                            cosine = base[row, 0, which : which + 1, lanes]
                            sine = base[row, 1, which : which + 1, lanes]
                            turned_re.append(real * cosine - imag * sine)
                            turned_im.append(real * sine + imag * cosine)
                        turned[held, lanes] = jnp.concatenate(turned_re, 0).astype(jnp.bfloat16)
                        turned[held, shifted] = jnp.concatenate(turned_im, 0).astype(jnp.bfloat16)
                values[: size * 48] = lax.dot_general(
                    turned[: size * 48],
                    table[row],
                    (((1,), (1,)), ((), ())),
                    preferred_element_type=jnp.float32,
                )

        def store(pair, inner):
            best = peak[...]
            for block in range(2):
                for side in range(2):
                    tile = pair * 4 + block * 2 + side
                    piece = values[
                        pl.ds(pl.multiple_of(pair * 48 + block * 24, 8), 24),
                        side * TILE : side * TILE + TILE,
                    ]
                    piece = jnp.where(column + tile * TILE < length, piece, 0.0)
                    rounded = piece.astype(jnp.bfloat16)
                    at_slot = slots[tile]
                    for field in range(3):
                        staged[at_slot // 6, row, at_slot % 6, field] = rounded[
                            field * 8 : field * 8 + 8
                        ]
                    best = jnp.maximum(best, rounded[:8].astype(jnp.float32))
            peak[...] = best
            return inner

        lax.fori_loop(0, pairs, store, 0)
        result(row).start()
        return carry

    lax.fori_loop(0, rows, one_row, 0)
    highest[...] = jnp.full((8, TILE), jnp.max(peak[...]))
    for row in range(rows):
        result(row).wait()


def fourier_stage(lengths, tile_slots, coeffs, table, base):
    rows = lengths.shape[0]
    scalar = pl.BlockSpec(memory_space=pltpu.SMEM)
    vmem = pl.BlockSpec(memory_space=pltpu.VMEM)
    hbm = pl.BlockSpec(memory_space=pl.ANY)
    return pl.pallas_call(
        fourier_kernel,
        in_specs=[scalar, scalar, vmem, vmem, vmem],
        out_specs=[hbm, vmem],
        scratch_shapes=[
            pltpu.VMEM((rows, 48, NM), jnp.float32),
            pltpu.VMEM((PAIRS * 48, 2 * NM), jnp.bfloat16),
            pltpu.VMEM((PAIRS * 48, SPAN), jnp.float32),
            pltpu.VMEM((8, TILE), jnp.float32),
            pltpu.VMEM((8, rows, 6, 3, 8, TILE), jnp.bfloat16),
            pltpu.SemaphoreType.DMA((rows,)),
        ],
        out_shape=[
            jax.ShapeDtypeStruct((8, rows, 6, 3, 8, TILE), jnp.bfloat16),
            jax.ShapeDtypeStruct((8, TILE), jnp.float32),
        ],
        compiler_params=pltpu.CompilerParams(vmem_limit_bytes=40 * MIB),
        cost_estimate=pl.CostEstimate(
            flops=rows * 576 * 2 * NM * 256, bytes_accessed=rows * SPAN * NM * 5, transcendentals=0
        ),
    )(lengths, tile_slots, coeffs, table, base)


def shards(spectral, legendre, derivative, wave_order, lat_order, row_lengths, tile_map):
    wave_index = lax.axis_index("wave")
    coeffs = legendre_stage(spectral, legendre, derivative, wave_order, lat_order)
    fourier = lax.all_to_all(coeffs, "wave", split_axis=0, concat_axis=0, tiled=True)

    row_ids = lax.dynamic_slice_in_dim(lat_order, wave_index * 8, 8)
    lengths = row_lengths[row_ids % 64]
    wave_row = wave_order.reshape(16, 5, GROUP).transpose(1, 0, 2).reshape(1, NM).astype(jnp.float32)
    table, base = table_stage(lengths, wave_row)
    tile_slots = jnp.zeros((48,), jnp.int32).at[tile_map].set(jnp.arange(48, dtype=jnp.int32))
    grid_part, highest = fourier_stage(lengths, tile_slots, fourier, table, base)
    received = lax.all_to_all(grid_part, "lev", split_axis=0, concat_axis=0, tiled=True)
    grid_values = received.transpose(1, 3, 0, 4, 2, 5).reshape(8, 3, 64, 768)
    highest = jnp.max(lax.all_gather(highest, "wave", axis=0), axis=0)
    hop = 1
    while hop < 8:
        pairs = [(at, at ^ hop) for at in range(8)]
        highest = jnp.maximum(highest, lax.ppermute(highest, "lev", pairs))
        hop *= 2
    return (grid_values, highest[0, 0])


def solution(mesh):
    placed = (
        P("wave", None, None, "lev", None),
        P("wave", None, None),
        P("wave", None, None),
        P(),
        P(),
        P(),
        P(),
    )
    return jax.shard_map(
        shards,
        mesh=mesh,
        in_specs=placed,
        out_specs=(P("wave", None, None, "lev"), P()),
        check_vma=False,
    )
```

```python
import functools

import jax
import jax.numpy as jnp
from jax import lax
from jax.experimental import pallas as pl
from jax.experimental.pallas import tpu as pltpu
from jax.sharding import PartitionSpec as P

NM = 1280
TILE = 128
GROUP = 16
SPAN = 256
BLOCKS = 24
PAIRS = 11
BATCH = 4
MIB = 1024 * 1024


def swap_lanes(parts, low_bit, lane):
    count = len(parts)
    bit = 1
    while bit < count:
        shift = bit * low_bit
        clear = (lane & shift) == 0
        fresh = list(parts)
        for at in range(count):
            if at & bit == 0:
                low, high = parts[at], parts[at | bit]
                fresh[at] = jnp.where(clear, low, pltpu.roll(high, shift, 1))
                fresh[at | bit] = jnp.where(clear, pltpu.roll(low, TILE - shift, 1), high)
        parts = fresh
        bit *= 2
    return parts


def legendre_kernel(
    all_waves, lat_row, spectral, legendre, derivative, out,
    spec_in, leg_in, der_in, sums, factor, permute, waves, order, spec_sem, leg_sem, der_sem,
):
    slots = spectral.shape[0]
    lane = lax.broadcasted_iota(jnp.int32, (48, TILE), 1)
    half = TILE // 2
    cuts = 4

    def copies(slot, cut):
        lanes = pl.ds(cut * SPAN, NM - cut * SPAN)
        return (
            pltpu.make_async_copy(
                legendre.at[slot, :, lanes], leg_in.at[slot, :, lanes], leg_sem.at[slot]
            ),
            pltpu.make_async_copy(
                derivative.at[slot, :, lanes], der_in.at[slot, :, lanes], der_sem.at[slot]
            ),
            pltpu.make_async_copy(
                spectral.at[slot, :, :, :, lanes], spec_in.at[slot, :, :, :, lanes], spec_sem.at[slot]
            ),
        )

    own = lax.axis_index("wave") * slots
    tally = jnp.int32(0)
    for slot in range(slots):
        wave = all_waves[own + slot]
        waves[slot] = wave
        tally = tally + lax.shift_left(jnp.int32(1), jnp.minimum(wave >> 8, cuts - 1) << 3)
    sizes = [(tally >> (8 * at)) & 127 for at in range(cuts)]
    begins = [None] * cuts
    total = jnp.int32(0)
    for at in reversed(range(cuts)):
        begins[at] = total
        total = total + sizes[at]
    places = sum(begins[at] << (8 * at) for at in range(cuts))
    for slot in range(slots):
        shift = jnp.minimum(waves[slot] >> 8, cuts - 1) << 3
        order[lax.shift_right_logical(places, shift) & 127] = slot
        places = places + lax.shift_left(jnp.int32(1), shift)

    for at in reversed(range(cuts)):

        def start(place, carry, at=at):
            for copy in copies(order[place], at):
                copy.start()
            return carry

        lax.fori_loop(begins[at], begins[at] + sizes[at], start, 0)

    number = lax.broadcasted_iota(jnp.int32, (8, NM), 1).astype(jnp.float32)
    factor[...] = jnp.where(number > 0, -float(NM) / jnp.maximum(number * (number + 1.0), 1.0), 0.0)
    down = lax.broadcasted_iota(jnp.int32, (TILE, TILE), 0)
    across = lax.broadcasted_iota(jnp.int32, (TILE, TILE), 1)
    at_row = jnp.where(down == lat_row[...], 1.0, 0.0).astype(jnp.bfloat16)
    at_lane = jnp.where(down == (across % 16) * 8 + across // 16, 1.0, 0.0).astype(jnp.bfloat16)
    permute[...] = jnp.dot(at_row, at_lane, preferred_element_type=jnp.float32).astype(jnp.bfloat16)

    for at in reversed(range(cuts)):
        first_lane = at * SPAN
        width = NM - first_lane
        end = begins[at] + sizes[at]

        def batch(step, carry, at=at, first_lane=first_lane, width=width, end=end):
            place = begins[at] + step * BATCH
            members = []
            for which in range(BATCH):
                slot = order[jnp.minimum(place + which, end - 1)]
                members.append(slot)

                @pl.when(place + which < end)
                def _(slot=slot):
                    for copy in copies(slot, at):
                        copy.wait()

            degree = lax.broadcasted_iota(jnp.int32, (8, width), 1) + first_lane
            scale = factor[:, first_lane:]
            results = []
            for slot in members:
                wave = waves[slot]
                live = degree >= wave
                odd = ((degree + wave) & 1) == 1
                keep_even = jnp.where(live & ~odd, 1.0, 0.0)
                keep_odd = jnp.where(live & odd, 1.0, 0.0)
                parts = [
                    spec_in[slot, field, side, :, first_lane:].astype(jnp.float32)
                    for field in range(2)
                    for side in range(2)
                ]
                rows = []
                for keep in (keep_even, keep_odd):
                    scaled = scale * keep
                    rows += [parts[0] * keep, parts[1] * keep]
                    rows += [part * scaled for part in parts]
                operand = jnp.concatenate(rows, axis=0).astype(jnp.bfloat16)
                both = jnp.concatenate(
                    [leg_in[slot, :, first_lane:], der_in[slot, :, first_lane:]], axis=0
                )
                results.append(
                    lax.dot_general(
                        operand, both, (((1,), (1,)), ((), ())), preferred_element_type=jnp.float32
                    )
                )
            for slot, result in zip(members, results):
                sums[slot] = result
            return carry

        lax.fori_loop(0, (sizes[at] + BATCH - 1) >> 2, batch, 0)

    left = lane < half

    def finish(group, carry):
        parts = []
        for at in range(GROUP):
            slot = group * GROUP + at
            wave_float = waves[slot].astype(jnp.float32)
            even_sum, odd_sum = sums[slot, :48], sums[slot, 48:]
            north = even_sum + odd_sum
            south = even_sum - odd_sum
            value = jnp.where(left, north, pltpu.roll(south, half, 1))
            slope = jnp.where(left, pltpu.roll(north, half, 1), -south)
            parts.append(
                jnp.concatenate(
                    [
                        value[0:8],
                        -wave_float * value[40:48] - slope[16:24],
                        -wave_float * value[24:32] + slope[32:40],
                        value[8:16],
                        wave_float * value[32:40] - slope[24:32],
                        wave_float * value[16:24] + slope[40:48],
                    ],
                    axis=0,
                ).astype(jnp.bfloat16)
            )
        placed = jnp.dot(
            jnp.concatenate(parts, axis=0), permute[...], preferred_element_type=jnp.float32
        )
        placed = placed.astype(jnp.bfloat16)
        parts = [placed[48 * at : 48 * at + 48] for at in range(GROUP)]
        for at, piece in enumerate(swap_lanes(parts, 1, lane)):
            out[at, group] = piece
        return carry

    lax.fori_loop(0, slots // GROUP, finish, 0)


def legendre_stage(spectral, legendre, derivative, wave_order, lat_order):
    slots = spectral.shape[0]
    groups = slots // GROUP
    hbm = pl.BlockSpec(memory_space=pl.ANY)
    vmem = pl.BlockSpec(memory_space=pltpu.VMEM)
    return pl.pallas_call(
        legendre_kernel,
        in_specs=[pl.BlockSpec(memory_space=pltpu.SMEM), vmem, hbm, hbm, hbm],
        out_specs=vmem,
        scratch_shapes=[
            pltpu.VMEM((slots, 2, 2, 8, NM), jnp.bfloat16),
            pltpu.VMEM((slots, 64, NM), jnp.bfloat16),
            pltpu.VMEM((slots, 64, NM), jnp.bfloat16),
            pltpu.VMEM((slots, 96, TILE), jnp.float32),
            pltpu.VMEM((8, NM), jnp.float32),
            pltpu.VMEM((TILE, TILE), jnp.bfloat16),
            pltpu.SMEM((slots,), jnp.int32),
            pltpu.SMEM((slots,), jnp.int32),
            pltpu.SemaphoreType.DMA((slots,)),
            pltpu.SemaphoreType.DMA((slots,)),
            pltpu.SemaphoreType.DMA((slots,)),
        ],
        out_shape=jax.ShapeDtypeStruct((16, groups, 48, TILE), jnp.bfloat16),
        compiler_params=pltpu.CompilerParams(vmem_limit_bytes=60 * MIB),
        cost_estimate=pl.CostEstimate(
            flops=slots * 96 * 128 * NM * 2, bytes_accessed=slots * 160 * NM * 2, transcendentals=0
        ),
    )(wave_order, lat_order.reshape(1, TILE), spectral, legendre, derivative)


def turn_parts(product, length, inverse):
    turned = product - jnp.floor(product * inverse) * length
    turn = turned * inverse
    quarter = jnp.floor(turn * 4.0 + 0.5)
    angle = (turn - quarter * 0.25) * 6.283185307179586
    square = angle * angle
    sine = angle * (1.0 + square * (-1.0 / 6 + square * (1.0 / 120 + square * (-1.0 / 5040))))
    cosine = 1.0 + square * (
        -0.5 + square * (1.0 / 24 + square * (-1.0 / 720 + square * (1.0 / 40320)))
    )
    which = quarter.astype(jnp.int32)
    odd = (which & 1) == 1
    cos_sign = jnp.where(((which + 1) & 2) == 0, 1.0, -1.0)
    sin_sign = jnp.where((which & 2) == 0, 1.0, -1.0)
    return cos_sign * jnp.where(odd, sine, cosine), sin_sign * jnp.where(odd, cosine, sine)


def table_kernel(lengths, waves, table, base):
    wave = waves[...]
    step = lax.broadcasted_iota(jnp.int32, (16, NM), 0).astype(jnp.float32)
    block = lax.broadcasted_iota(jnp.int32, (BLOCKS, NM), 0).astype(jnp.float32)

    def one_row(row, carry):
        length = lengths[row].astype(jnp.float32)
        inverse = (1.0 / jnp.full((8, NM), length))[:1]
        fine_cos, fine_sin = turn_parts(step * wave, length, inverse)
        coarse_cos, coarse_sin = turn_parts(step * wave * 16.0, length, inverse)
        for at in range(16):
            one_cos, one_sin = coarse_cos[at : at + 1], coarse_sin[at : at + 1]
            span = slice(16 * at, 16 * at + 16)
            table[row, span, :NM] = (one_cos * fine_cos - one_sin * fine_sin).astype(jnp.bfloat16)
            table[row, span, NM:] = (-one_sin * fine_cos - one_cos * fine_sin).astype(jnp.bfloat16)
        base_cos, base_sin = turn_parts(block * wave * float(SPAN), length, inverse)
        weight = jnp.where(wave == 0.0, 1.0, 2.0) * jnp.where(2.0 * wave < length, 1.0, 0.0)
        base[row, 0] = base_cos * weight
        base[row, 1] = base_sin * weight
        return carry

    lax.fori_loop(0, table.shape[0], one_row, 0)


def table_stage(lengths, wave_row):
    rows = lengths.shape[0]
    vmem = pl.BlockSpec(memory_space=pltpu.VMEM)
    return pl.pallas_call(
        table_kernel,
        in_specs=[pl.BlockSpec(memory_space=pltpu.SMEM), vmem],
        out_specs=[vmem, vmem],
        out_shape=[
            jax.ShapeDtypeStruct((rows, SPAN, 2 * NM), jnp.bfloat16),
            jax.ShapeDtypeStruct((rows, 2, BLOCKS, NM), jnp.float32),
        ],
        compiler_params=pltpu.CompilerParams(vmem_limit_bytes=30 * MIB),
        cost_estimate=pl.CostEstimate(
            flops=rows * SPAN * NM * 40, bytes_accessed=rows * SPAN * NM * 5, transcendentals=0
        ),
    )(lengths, wave_row)


def fourier_kernel(
    lengths, slots, coeffs, table, base, out, highest,
    fields, turned, values, peak, staged, out_sem,
):
    rows = table.shape[0]
    lane = lax.broadcasted_iota(jnp.int32, (48, TILE), 1)
    column = lax.broadcasted_iota(jnp.int32, (24, TILE), 1)

    def result(row):
        return pltpu.make_async_copy(staged.at[:, row], out.at[:, row], out_sem.at[row])

    peak[...] = jnp.zeros_like(peak)
    for group in range(5):
        for half in range(2):
            parts = [coeffs[half * 8 + at, group] for at in range(8)]
            tile = group * 2 + half
            for at, block in enumerate(swap_lanes(parts, 16, lane)):
                fields[at, :, tile * TILE : tile * TILE + TILE] = block.astype(jnp.float32)

    def one_row(row, carry):
        length = lengths[row]
        pairs = (length + 2 * SPAN - 1) >> 9
        staged[:, row] = jnp.zeros((8, 6, 3, 8, TILE), jnp.bfloat16)
        sizes = (2, 4, 6, 8, PAIRS)
        for at, size in enumerate(sizes):
            above = pairs > sizes[at - 1] if at else pairs > 0

            @pl.when(above & (pairs <= size))
            def _(size=size):
                for chunk in range(5):
                    lanes = slice(chunk * 256, chunk * 256 + 256)
                    shifted = slice(NM + chunk * 256, NM + chunk * 256 + 256)
                    real = fields[row, 0:24, lanes]
                    imag = fields[row, 24:48, lanes]
                    for pair in range(size):
                        held = slice(pair * 48, pair * 48 + 48)
                        turned_re, turned_im = [], []
                        for side in range(2):
                            which = pair * 2 + side
                            cosine = base[row, 0, which : which + 1, lanes]
                            sine = base[row, 1, which : which + 1, lanes]
                            turned_re.append(real * cosine - imag * sine)
                            turned_im.append(real * sine + imag * cosine)
                        turned[held, lanes] = jnp.concatenate(turned_re, 0).astype(jnp.bfloat16)
                        turned[held, shifted] = jnp.concatenate(turned_im, 0).astype(jnp.bfloat16)
                values[: size * 48] = lax.dot_general(
                    turned[: size * 48],
                    table[row],
                    (((1,), (1,)), ((), ())),
                    preferred_element_type=jnp.float32,
                )

        def store(pair, inner):
            best = peak[...]
            for block in range(2):
                for side in range(2):
                    tile = pair * 4 + block * 2 + side
                    piece = values[
                        pl.ds(pl.multiple_of(pair * 48 + block * 24, 8), 24),
                        side * TILE : side * TILE + TILE,
                    ]
                    piece = jnp.where(column + tile * TILE < length, piece, 0.0)
                    rounded = piece.astype(jnp.bfloat16)
                    owner, place = slots[0, tile], slots[1, tile]
                    for field in range(3):
                        staged[owner, row, place, field] = rounded[field * 8 : field * 8 + 8]
                    best = jnp.maximum(best, rounded[:8].astype(jnp.float32))
            peak[...] = best
            return inner

        lax.fori_loop(0, pairs, store, 0)
        result(row).start()
        return carry

    lax.fori_loop(0, rows, one_row, 0)
    highest[...] = jnp.full((8, TILE), jnp.max(peak[...]))
    for row in range(rows):
        result(row).wait()


def fourier_stage(lengths, tile_slots, coeffs, table, base):
    rows = lengths.shape[0]
    scalar = pl.BlockSpec(memory_space=pltpu.SMEM)
    vmem = pl.BlockSpec(memory_space=pltpu.VMEM)
    hbm = pl.BlockSpec(memory_space=pl.ANY)
    return pl.pallas_call(
        fourier_kernel,
        in_specs=[scalar, scalar, vmem, vmem, vmem],
        out_specs=[hbm, vmem],
        scratch_shapes=[
            pltpu.VMEM((rows, 48, NM), jnp.float32),
            pltpu.VMEM((PAIRS * 48, 2 * NM), jnp.bfloat16),
            pltpu.VMEM((PAIRS * 48, SPAN), jnp.float32),
            pltpu.VMEM((8, TILE), jnp.float32),
            pltpu.VMEM((8, rows, 6, 3, 8, TILE), jnp.bfloat16),
            pltpu.SemaphoreType.DMA((rows,)),
        ],
        out_shape=[
            jax.ShapeDtypeStruct((8, rows, 6, 3, 8, TILE), jnp.bfloat16),
            jax.ShapeDtypeStruct((8, TILE), jnp.float32),
        ],
        compiler_params=pltpu.CompilerParams(vmem_limit_bytes=40 * MIB),
        cost_estimate=pl.CostEstimate(
            flops=rows * 576 * 2 * NM * 256, bytes_accessed=rows * SPAN * NM * 5, transcendentals=0
        ),
    )(lengths, tile_slots, coeffs, table, base)


def shards(spectral, legendre, derivative, wave_order, lat_order, row_lengths, tile_map):
    wave_index = lax.axis_index("wave")
    coeffs = legendre_stage(spectral, legendre, derivative, wave_order, lat_order)
    fourier = lax.all_to_all(coeffs, "wave", split_axis=0, concat_axis=0, tiled=True)

    row_ids = lax.dynamic_slice_in_dim(lat_order, wave_index * 8, 8)
    lengths = row_lengths[row_ids % 64]
    wave_row = wave_order.reshape(16, 5, GROUP).transpose(1, 0, 2).reshape(1, NM).astype(jnp.float32)
    table, base = table_stage(lengths, wave_row)
    tile_slots = jnp.zeros((48,), jnp.int32).at[tile_map].set(jnp.arange(48, dtype=jnp.int32))
    tile_slots = jnp.stack([tile_slots // 6, tile_slots % 6])
    grid_part, highest = fourier_stage(lengths, tile_slots, fourier, table, base)
    received = lax.all_to_all(grid_part, "lev", split_axis=0, concat_axis=0, tiled=True)
    grid_values = received.transpose(1, 3, 0, 4, 2, 5).reshape(8, 3, 64, 768)
    highest = jnp.max(lax.all_gather(highest, "wave", axis=0), axis=0)
    hop = 1
    while hop < 8:
        pairs = [(at, at ^ hop) for at in range(8)]
        highest = jnp.maximum(highest, lax.ppermute(highest, "lev", pairs))
        hop *= 2
    return (grid_values, highest[0, 0])


def solution(mesh):
    placed = (
        P("wave", None, None, "lev", None),
        P("wave", None, None),
        P("wave", None, None),
        P(),
        P(),
        P(),
        P(),
    )
    return jax.shard_map(
        shards,
        mesh=mesh,
        in_specs=placed,
        out_specs=(P("wave", None, None, "lev"), P()),
        check_vma=False,
    )
```

```python
import functools

import jax
import jax.numpy as jnp
from jax import lax
from jax.experimental import pallas as pl
from jax.experimental.pallas import tpu as pltpu
from jax.sharding import PartitionSpec as P

NM = 1280
TILE = 128
GROUP = 16
SPAN = 256
BLOCKS = 24
PAIRS = 11
BATCH = 4
MIB = 1024 * 1024


def swap_lanes(parts, low_bit, lane):
    count = len(parts)
    bit = 1
    while bit < count:
        shift = bit * low_bit
        clear = (lane & shift) == 0
        fresh = list(parts)
        for at in range(count):
            if at & bit == 0:
                low, high = parts[at], parts[at | bit]
                fresh[at] = jnp.where(clear, low, pltpu.roll(high, shift, 1))
                fresh[at | bit] = jnp.where(clear, pltpu.roll(low, TILE - shift, 1), high)
        parts = fresh
        bit *= 2
    return parts


def legendre_kernel(
    all_waves, lat_row, spectral, legendre, derivative, out,
    spec_in, leg_in, der_in, sums, factor, permute, waves, order, spec_sem, leg_sem, der_sem,
):
    slots = spectral.shape[0]
    lane = lax.broadcasted_iota(jnp.int32, (48, TILE), 1)
    half = TILE // 2
    cuts = 4

    def copies(slot, cut):
        lanes = pl.ds(cut * SPAN, NM - cut * SPAN)
        return (
            pltpu.make_async_copy(
                legendre.at[slot, :, lanes], leg_in.at[slot, :, lanes], leg_sem.at[slot]
            ),
            pltpu.make_async_copy(
                derivative.at[slot, :, lanes], der_in.at[slot, :, lanes], der_sem.at[slot]
            ),
            pltpu.make_async_copy(
                spectral.at[slot, :, :, :, lanes], spec_in.at[slot, :, :, :, lanes], spec_sem.at[slot]
            ),
        )

    own = lax.axis_index("wave") * slots
    tally = jnp.int32(0)
    for slot in range(slots):
        wave = all_waves[own + slot]
        waves[slot] = wave
        tally = tally + lax.shift_left(jnp.int32(1), jnp.minimum(wave >> 8, cuts - 1) << 3)
    sizes = [(tally >> (8 * at)) & 127 for at in range(cuts)]
    begins = [None] * cuts
    total = jnp.int32(0)
    for at in reversed(range(cuts)):
        begins[at] = total
        total = total + sizes[at]
    places = sum(begins[at] << (8 * at) for at in range(cuts))
    for slot in range(slots):
        shift = jnp.minimum(waves[slot] >> 8, cuts - 1) << 3
        order[lax.shift_right_logical(places, shift) & 127] = slot
        places = places + lax.shift_left(jnp.int32(1), shift)

    for at in reversed(range(cuts)):

        def start(place, carry, at=at):
            for copy in copies(order[place], at):
                copy.start()
            return carry

        lax.fori_loop(begins[at], begins[at] + sizes[at], start, 0)

    number = lax.broadcasted_iota(jnp.int32, (8, NM), 1).astype(jnp.float32)
    factor[...] = jnp.where(number > 0, -float(NM) / jnp.maximum(number * (number + 1.0), 1.0), 0.0)
    down = lax.broadcasted_iota(jnp.int32, (TILE, TILE), 0)
    across = lax.broadcasted_iota(jnp.int32, (TILE, TILE), 1)
    at_row = jnp.where(down == lat_row[...], 1.0, 0.0).astype(jnp.bfloat16)
    at_lane = jnp.where(down == (across % 16) * 8 + across // 16, 1.0, 0.0).astype(jnp.bfloat16)
    permute[...] = jnp.dot(at_row, at_lane, preferred_element_type=jnp.float32).astype(jnp.bfloat16)

    for at in reversed(range(cuts)):
        first_lane = at * SPAN
        width = NM - first_lane
        end = begins[at] + sizes[at]

        def batch(step, carry, at=at, first_lane=first_lane, width=width, end=end):
            place = begins[at] + step * BATCH
            members = []
            for which in range(BATCH):
                slot = order[jnp.minimum(place + which, end - 1)]
                members.append(slot)

                @pl.when(place + which < end)
                def _(slot=slot):
                    for copy in copies(slot, at):
                        copy.wait()

            degree = lax.broadcasted_iota(jnp.int32, (8, width), 1) + first_lane
            scale = factor[:, first_lane:]
            results = []
            for slot in members:
                wave = waves[slot]
                live = degree >= wave
                odd = ((degree + wave) & 1) == 1
                keep_even = jnp.where(live & ~odd, 1.0, 0.0)
                keep_odd = jnp.where(live & odd, 1.0, 0.0)
                parts = [
                    spec_in[slot, field, side, :, first_lane:].astype(jnp.float32)
                    for field in range(2)
                    for side in range(2)
                ]
                rows = []
                for keep in (keep_even, keep_odd):
                    scaled = scale * keep
                    rows += [parts[0] * keep, parts[1] * keep]
                    rows += [part * scaled for part in parts]
                operand = jnp.concatenate(rows, axis=0).astype(jnp.bfloat16)
                both = jnp.concatenate(
                    [leg_in[slot, :, first_lane:], der_in[slot, :, first_lane:]], axis=0
                )
                results.append(
                    lax.dot_general(
                        operand, both, (((1,), (1,)), ((), ())), preferred_element_type=jnp.float32
                    )
                )
            for slot, result in zip(members, results):
                sums[slot] = result
            return carry

        lax.fori_loop(0, (sizes[at] + BATCH - 1) >> 2, batch, 0)

    left = lane < half

    def finish(group, carry):
        parts = []
        for at in range(GROUP):
            slot = group * GROUP + at
            wave_float = waves[slot].astype(jnp.float32)
            even_sum, odd_sum = sums[slot, :48], sums[slot, 48:]
            north = even_sum + odd_sum
            south = even_sum - odd_sum
            value = jnp.where(left, north, pltpu.roll(south, half, 1))
            slope = jnp.where(left, pltpu.roll(north, half, 1), -south)
            parts.append(
                jnp.concatenate(
                    [
                        value[0:8],
                        -wave_float * value[40:48] - slope[16:24],
                        -wave_float * value[24:32] + slope[32:40],
                        value[8:16],
                        wave_float * value[32:40] - slope[24:32],
                        wave_float * value[16:24] + slope[40:48],
                    ],
                    axis=0,
                ).astype(jnp.bfloat16)
            )
        placed = jnp.dot(
            jnp.concatenate(parts, axis=0), permute[...], preferred_element_type=jnp.float32
        )
        placed = placed.astype(jnp.bfloat16)
        parts = [placed[48 * at : 48 * at + 48] for at in range(GROUP)]
        for at, piece in enumerate(swap_lanes(parts, 1, lane)):
            out[at, group] = piece
        return carry

    lax.fori_loop(0, slots // GROUP, finish, 0)


def legendre_stage(spectral, legendre, derivative, wave_order, lat_order):
    slots = spectral.shape[0]
    groups = slots // GROUP
    hbm = pl.BlockSpec(memory_space=pl.ANY)
    vmem = pl.BlockSpec(memory_space=pltpu.VMEM)
    return pl.pallas_call(
        legendre_kernel,
        in_specs=[pl.BlockSpec(memory_space=pltpu.SMEM), vmem, hbm, hbm, hbm],
        out_specs=vmem,
        scratch_shapes=[
            pltpu.VMEM((slots, 2, 2, 8, NM), jnp.bfloat16),
            pltpu.VMEM((slots, 64, NM), jnp.bfloat16),
            pltpu.VMEM((slots, 64, NM), jnp.bfloat16),
            pltpu.VMEM((slots, 96, TILE), jnp.float32),
            pltpu.VMEM((8, NM), jnp.float32),
            pltpu.VMEM((TILE, TILE), jnp.bfloat16),
            pltpu.SMEM((slots,), jnp.int32),
            pltpu.SMEM((slots,), jnp.int32),
            pltpu.SemaphoreType.DMA((slots,)),
            pltpu.SemaphoreType.DMA((slots,)),
            pltpu.SemaphoreType.DMA((slots,)),
        ],
        out_shape=jax.ShapeDtypeStruct((16, groups, 48, TILE), jnp.bfloat16),
        compiler_params=pltpu.CompilerParams(vmem_limit_bytes=60 * MIB),
        cost_estimate=pl.CostEstimate(
            flops=slots * 96 * 128 * NM * 2, bytes_accessed=slots * 160 * NM * 2, transcendentals=0
        ),
    )(wave_order, lat_order.reshape(1, TILE), spectral, legendre, derivative)


def turn_parts(product, length, inverse):
    turned = product - jnp.floor(product * inverse) * length
    turn = turned * inverse
    quarter = jnp.floor(turn * 4.0 + 0.5)
    angle = (turn - quarter * 0.25) * 6.283185307179586
    square = angle * angle
    sine = angle * (1.0 + square * (-1.0 / 6 + square * (1.0 / 120 + square * (-1.0 / 5040))))
    cosine = 1.0 + square * (
        -0.5 + square * (1.0 / 24 + square * (-1.0 / 720 + square * (1.0 / 40320)))
    )
    which = quarter.astype(jnp.int32)
    odd = (which & 1) == 1
    cos_sign = jnp.where(((which + 1) & 2) == 0, 1.0, -1.0)
    sin_sign = jnp.where((which & 2) == 0, 1.0, -1.0)
    return cos_sign * jnp.where(odd, sine, cosine), sin_sign * jnp.where(odd, cosine, sine)


def table_kernel(lengths, waves, table, base):
    wave = waves[...]
    step = lax.broadcasted_iota(jnp.int32, (16, NM), 0).astype(jnp.float32)
    block = lax.broadcasted_iota(jnp.int32, (BLOCKS, NM), 0).astype(jnp.float32)

    def one_row(row, carry):
        length = lengths[row].astype(jnp.float32)
        inverse = (1.0 / jnp.full((8, NM), length))[:1]
        fine_cos, fine_sin = turn_parts(step * wave, length, inverse)
        coarse_cos, coarse_sin = turn_parts(step * wave * 16.0, length, inverse)
        for at in range(16):
            one_cos, one_sin = coarse_cos[at : at + 1], coarse_sin[at : at + 1]
            span = slice(16 * at, 16 * at + 16)
            table[row, span, :NM] = (one_cos * fine_cos - one_sin * fine_sin).astype(jnp.bfloat16)
            table[row, span, NM:] = (-one_sin * fine_cos - one_cos * fine_sin).astype(jnp.bfloat16)
        base_cos, base_sin = turn_parts(block * wave * float(SPAN), length, inverse)
        weight = jnp.where(wave == 0.0, 1.0, 2.0) * jnp.where(2.0 * wave < length, 1.0, 0.0)
        base[row, 0] = base_cos * weight
        base[row, 1] = base_sin * weight
        return carry

    lax.fori_loop(0, table.shape[0], one_row, 0)


def table_stage(lengths, wave_row):
    rows = lengths.shape[0]
    vmem = pl.BlockSpec(memory_space=pltpu.VMEM)
    return pl.pallas_call(
        table_kernel,
        in_specs=[pl.BlockSpec(memory_space=pltpu.SMEM), vmem],
        out_specs=[vmem, vmem],
        out_shape=[
            jax.ShapeDtypeStruct((rows, SPAN, 2 * NM), jnp.bfloat16),
            jax.ShapeDtypeStruct((rows, 2, BLOCKS, NM), jnp.float32),
        ],
        compiler_params=pltpu.CompilerParams(vmem_limit_bytes=30 * MIB),
        cost_estimate=pl.CostEstimate(
            flops=rows * SPAN * NM * 40, bytes_accessed=rows * SPAN * NM * 5, transcendentals=0
        ),
    )(lengths, wave_row)


def fourier_kernel(
    lengths, slots, coeffs, table, base, out, highest,
    fields, turned, values, peak, staged, out_sem,
):
    rows = table.shape[0]
    lane = lax.broadcasted_iota(jnp.int32, (48, TILE), 1)
    column = lax.broadcasted_iota(jnp.int32, (24, TILE), 1)

    def result(row):
        return pltpu.make_async_copy(staged.at[:, row], out.at[:, row], out_sem.at[row])

    peak[...] = jnp.zeros_like(peak)
    for group in range(5):
        for half in range(2):
            parts = [coeffs[half * 8 + at, group] for at in range(8)]
            tile = group * 2 + half
            for at, block in enumerate(swap_lanes(parts, 16, lane)):
                fields[at, :, tile * TILE : tile * TILE + TILE] = block.astype(jnp.float32)

    def one_row(row, carry):
        length = lengths[row]
        pairs = (length + 2 * SPAN - 1) >> 9
        staged[:, row] = jnp.zeros((8, 6, 3, 8, TILE), jnp.bfloat16)
        sizes = (2, 4, 6, 8, PAIRS)
        for at, size in enumerate(sizes):
            above = pairs > sizes[at - 1] if at else pairs > 0

            @pl.when(above & (pairs <= size))
            def _(size=size):
                for chunk in range(5):
                    lanes = slice(chunk * 256, chunk * 256 + 256)
                    shifted = slice(NM + chunk * 256, NM + chunk * 256 + 256)
                    real = fields[row, 0:24, lanes]
                    imag = fields[row, 24:48, lanes]
                    for pair in range(size):
                        held = slice(pair * 48, pair * 48 + 48)
                        turned_re, turned_im = [], []
                        for side in range(2):
                            which = pair * 2 + side
                            cosine = base[row, 0, which : which + 1, lanes]
                            sine = base[row, 1, which : which + 1, lanes]
                            turned_re.append(real * cosine - imag * sine)
                            turned_im.append(real * sine + imag * cosine)
                        turned[held, lanes] = jnp.concatenate(turned_re, 0).astype(jnp.bfloat16)
                        turned[held, shifted] = jnp.concatenate(turned_im, 0).astype(jnp.bfloat16)
                values[: size * 48] = lax.dot_general(
                    turned[: size * 48],
                    table[row],
                    (((1,), (1,)), ((), ())),
                    preferred_element_type=jnp.float32,
                )

        def store(pair, inner):
            best = peak[...]
            for block in range(2):
                for side in range(2):
                    tile = pair * 4 + block * 2 + side
                    piece = values[
                        pl.ds(pl.multiple_of(pair * 48 + block * 24, 8), 24),
                        side * TILE : side * TILE + TILE,
                    ]
                    piece = jnp.where(column + tile * TILE < length, piece, 0.0)
                    rounded = piece.astype(jnp.bfloat16)
                    owner, place = slots[0, tile], slots[1, tile]
                    for field in range(3):
                        staged[owner, row, place, field] = rounded[field * 8 : field * 8 + 8]
                    best = jnp.maximum(best, rounded[:8].astype(jnp.float32))
            peak[...] = best
            return inner

        lax.fori_loop(0, pairs, store, 0)
        result(row).start()
        return carry

    lax.fori_loop(0, rows, one_row, 0)
    highest[...] = jnp.full((8, TILE), jnp.max(peak[...]))
    for row in range(rows):
        result(row).wait()


def fourier_stage(lengths, tile_slots, coeffs, table, base):
    rows = lengths.shape[0]
    scalar = pl.BlockSpec(memory_space=pltpu.SMEM)
    vmem = pl.BlockSpec(memory_space=pltpu.VMEM)
    hbm = pl.BlockSpec(memory_space=pl.ANY)
    return pl.pallas_call(
        fourier_kernel,
        in_specs=[scalar, scalar, vmem, vmem, vmem],
        out_specs=[hbm, vmem],
        scratch_shapes=[
            pltpu.VMEM((rows, 48, NM), jnp.float32),
            pltpu.VMEM((PAIRS * 48, 2 * NM), jnp.bfloat16),
            pltpu.VMEM((PAIRS * 48, SPAN), jnp.float32),
            pltpu.VMEM((8, TILE), jnp.float32),
            pltpu.VMEM((8, rows, 6, 3, 8, TILE), jnp.bfloat16),
            pltpu.SemaphoreType.DMA((rows,)),
        ],
        out_shape=[
            jax.ShapeDtypeStruct((8, rows, 6, 3, 8, TILE), jnp.bfloat16),
            jax.ShapeDtypeStruct((8, TILE), jnp.float32),
        ],
        compiler_params=pltpu.CompilerParams(vmem_limit_bytes=40 * MIB),
        cost_estimate=pl.CostEstimate(
            flops=rows * 576 * 2 * NM * 256, bytes_accessed=rows * SPAN * NM * 5, transcendentals=0
        ),
    )(lengths, tile_slots, coeffs, table, base)


def shards(spectral, legendre, derivative, wave_order, lat_order, row_lengths, tile_map):
    wave_index = lax.axis_index("wave")
    coeffs = legendre_stage(spectral, legendre, derivative, wave_order, lat_order)
    fourier = lax.all_to_all(coeffs, "wave", split_axis=0, concat_axis=0, tiled=True)

    row_ids = lax.dynamic_slice_in_dim(lat_order, wave_index * 8, 8)
    lengths = row_lengths[row_ids % 64]
    wave_row = wave_order.reshape(16, 5, GROUP).transpose(1, 0, 2).reshape(1, NM).astype(jnp.float32)
    table, base = table_stage(lengths, wave_row)
    tile_slots = jnp.zeros((48,), jnp.int32).at[tile_map].set(jnp.arange(48, dtype=jnp.int32))
    tile_slots = jnp.stack([tile_slots // 6, tile_slots % 6])
    grid_part, highest = fourier_stage(lengths, tile_slots, fourier, table, base)
    received = lax.all_to_all(grid_part, "lev", split_axis=0, concat_axis=0, tiled=True)
    grid_values = received.transpose(1, 3, 0, 4, 2, 5).reshape(8, 3, 64, 768)
    highest = jnp.max(lax.all_gather(highest, "wave", axis=0), axis=0)
    for hop in (4, 2, 1):
        pairs = [(at, at ^ hop) for at in range(8)]
        highest = jnp.maximum(highest, lax.ppermute(highest, "lev", pairs))
    return (grid_values, highest[0, 0])


def solution(mesh):
    placed = (
        P("wave", None, None, "lev", None),
        P("wave", None, None),
        P("wave", None, None),
        P(),
        P(),
        P(),
        P(),
    )
    return jax.shard_map(
        shards,
        mesh=mesh,
        in_specs=placed,
        out_specs=(P("wave", None, None, "lev"), P()),
        check_vma=False,
    )
```
